256 devices in a mesh: band: 8 (over y, x_hi), pw: 32 (over x_lo, z, core).
Axes of the slice: x: 4 (x_hi: 2, x_lo: 2; x = x_hi * 2 + x_lo), y: 4, z: 8, core: 2. Of those that a mesh axis runs over, the one named last changes fastest.
Arguments:
- orbitals: bfloat16 [256, 96, 96, 96], P('band', 'pw'), may hold values from -6 to 6
- owners: int32 [4], replicated, may hold values from 0 to 7, as said below
- chosen: int32 [4, 2], replicated, may hold values from 0 to 31
- shell_index: int32 [96, 96, 96], P(None, 'pw'), may hold values from 0 to 127
- shell_kernel: float32 [128], replicated, may hold values from 0.1 to 1
Outputs:
- applied: bfloat16 [256, 96, 96, 96], P('band', 'pw')
The draws below stay inside these ranges and needn't reach their ends.
Inputs may be any that keep to these rules, and one draw needn't show every extreme that they name: The owners of different rounds are different band groups.
All inputs are finite; a program needn't handle non-finite values.
Results may differ from the reference program's by a relative error of at most 0.012.
Values may be sent and summed in bfloat16 or wider, within the bound.
No kernel may reach another device: no remote copies, remote signals or barrier semaphores. Data moves between devices by JAX's collectives and lax.ppermute only.
A program may use at most 192 MiB of HBM per device.

```python
import math
import jax
import jax.numpy as jnp
from jax import lax

GRID = 96
SOURCES = 2
ROUNDS = 4
LEVELS = 128
GROUP_ORBS = 32
ALL_ORBS = 256
N_BAND = 8


def draw_owners(key, part):
    key = jax.random.fold_in(key, 11)
    shuffled = jax.random.permutation(key, lax.iota(jnp.int32, N_BAND))
    return shuffled[:ROUNDS].astype(jnp.int32)


def touch_ends(array, key, smallest, top_value):
    longest = array.shape.index(max(array.shape))
    spots = []
    for shift in (0, 1):
        where = [jax.random.randint(jax.random.fold_in(key, axis), (), 0, length) for axis, length in enumerate(array.shape)]
        where[longest] = (where[longest] + shift) % array.shape[longest]
        spots.append(tuple(where))
    return array.at[spots[0]].set(smallest).at[spots[1]].set(top_value)


def block_levels(stream_key, shape, cuts, low, high):
    factor_of = 1.0
    for dim, parts in cuts:
        draws = jax.random.uniform(jax.random.fold_in(jax.random.fold_in(stream_key, 6), dim), (parts,), jnp.float32, low / len(cuts), high / len(cuts))
        factor_of = factor_of * jnp.repeat(jnp.exp(draws), shape[dim] // parts).reshape((-1,) + (1,) * (len(shape) - 1 - dim))
    return factor_of


def noise(rng, shape, deviation, limit, cuts=(), kind=jnp.bfloat16):
    array = jax.random.normal(rng, shape, jnp.float32) * deviation
    if len(cuts) > 0:
        array = block_levels(rng, shape, cuts, -0.22, 0.18) * array
    return jnp.clip(array, min=-limit, max=limit).astype(kind)


def setup_inputs(seed: int = 0) -> dict:
    streams_of = jax.random.split(jax.random.key(seed), 6)
    return {
        "orbitals": noise(streams_of[0], (ALL_ORBS, GRID, GRID, GRID), 1.0, 6.0, ((0, 8), (1, 32))),
        "owners": draw_owners(jax.random.fold_in(streams_of[5], 71), 0),
        "chosen": touch_ends(jax.random.randint(streams_of[2], (ROUNDS, SOURCES), 0, GROUP_ORBS), jax.random.fold_in(streams_of[2], 1), 0, GROUP_ORBS - 1).astype(jnp.int32),
        "shell_index": touch_ends(jax.random.randint(streams_of[3], (GRID, GRID, GRID), 0, LEVELS), jax.random.fold_in(streams_of[3], 1), 0, LEVELS - 1).astype(jnp.int32),
        "shell_kernel": jnp.clip(jnp.exp(jax.random.uniform(streams_of[4], (LEVELS,), jnp.float32, math.log(0.1), math.log(1.0))), 0.1, 1.0),
    }


EXCHANGE_FRACTION = 0.25

def cas_table(length):
    counter = lax.iota(jnp.int32, length)
    product = counter[:, None] * counter[None, :] % length
    angles = product.astype(jnp.float32) * (2.0 * math.pi / length)
    return ((jnp.cos(angles) + jnp.sin(angles)) / math.sqrt(length)).astype(jnp.bfloat16)

def solve_pair(pair_data, wide_table, kernel):
    section = jnp.einsum('xyz,kz->xyk', pair_data.astype(jnp.float32), wide_table).astype(jnp.bfloat16)
    section = jnp.einsum('xyz,ky->xkz', section.astype(jnp.float32), wide_table).astype(jnp.bfloat16)
    section = (kernel * jnp.einsum('xyz,kx->kyz', section.astype(jnp.float32), wide_table)).astype(jnp.bfloat16)
    section = jnp.einsum('xyz,kx->kyz', section.astype(jnp.float32), wide_table).astype(jnp.bfloat16)
    section = jnp.einsum('xyz,kz->xyk', section.astype(jnp.float32), wide_table).astype(jnp.bfloat16)
    return jnp.einsum('xyz,ky->xkz', section.astype(jnp.float32), wide_table)

def reference(orbitals, owners, chosen, shell_index, shell_kernel):
    length = orbitals.shape[1]
    wide_table = cas_table(length).astype(jnp.float32)
    kernel = shell_kernel[shell_index]
    rows = (owners[:, None].astype(jnp.int32) * GROUP_ORBS + chosen.astype(jnp.int32)).reshape(-1)
    sources = orbitals[rows]

    def one_target(target):

        def add_source(summed, source):
            pair_data = (source.astype(jnp.float32) * target.astype(jnp.float32)).astype(jnp.bfloat16)
            potential = solve_pair(pair_data, wide_table, kernel)
            return (summed + source.astype(jnp.float32) * potential, None)
        start = jnp.zeros(target.shape, jnp.float32)
        summed, unused = lax.scan(add_source, start, sources)
        return (-EXCHANGE_FRACTION * summed).astype(jnp.bfloat16)
    return lax.map(one_target, orbitals)
```

```python
import math

import jax
import jax.numpy as jnp
from jax import lax
from jax.experimental import pallas as pl
from jax.experimental.pallas import tpu as pltpu
from jax.sharding import PartitionSpec as P

F32 = jnp.float32
BF16 = jnp.bfloat16
EXCHANGE_FRACTION = 0.25
LANES = 128
VMEM_LIMIT = 60 * 2**20
PITCH = 104


def cas_table(length):
    counter = lax.iota(jnp.int32, length)
    product = counter[:, None] * counter[None, :] % length
    angles = product.astype(F32) * (2.0 * math.pi / length)
    return ((jnp.cos(angles) + jnp.sin(angles)) / math.sqrt(length)).astype(BF16)


def double_table(table):
    length = table.shape[0]
    wide = jnp.zeros((2 * LANES, 2 * LANES), table.dtype)
    wide = wide.at[:length, :length].set(table)
    return wide.at[LANES : LANES + length, LANES : LANES + length].set(table)


def dot(a, b):
    return jnp.dot(a, b, preferred_element_type=F32)


def lookup_kernel(level_ref, values_ref, field_ref):
    parts, _, planes, length, width = level_ref.shape

    @pl.loop(0, parts)
    def _(part):
        for plane in range(planes):
            levels = level_ref[part, 0, plane].astype(F32).astype(jnp.int32)
            levels = jnp.concatenate([levels, jnp.zeros((length, LANES - width), jnp.int32)], axis=1)
            values = jnp.broadcast_to(values_ref[...], (length, LANES))
            field_ref[part * planes + plane] = jnp.take_along_axis(values, levels, axis=1)


def kernel_field(gathered, shell_kernel):
    parts, count, planes, length, width = gathered.shape
    return pl.pallas_call(
        lookup_kernel,
        grid=(1,),
        in_specs=[
            pl.BlockSpec((parts, 1, planes, length, width), lambda i: (0, count - 1, 0, 0, 0)),
            pl.BlockSpec((1, LANES), lambda i: (0, 0)),
        ],
        out_specs=pl.BlockSpec((parts * planes, length, LANES), lambda i: (0, 0, 0)),
        out_shape=jax.ShapeDtypeStruct((parts * planes, length, LANES), F32),
        compiler_params=pltpu.CompilerParams(vmem_limit_bytes=VMEM_LIMIT),
        name="kernel_field",
    )(gathered, shell_kernel.reshape(1, LANES))


def solve_kernel(orbital_ref, source_ref, field_ref, table_ref, double_ref, out_ref, first, second, total):
    parts, planes, length, width = orbital_ref.shape
    grid_step = pl.program_id(0)
    group = 8 * planes
    middle_group = 24
    table = table_ref[...]
    halves = (slice(0, LANES), slice(LANES, 2 * LANES))
    blank = jnp.zeros((length, LANES - width), BF16)

    @pl.when(grid_step == 0)
    def _():
        total[...] = jnp.zeros_like(total)

    @pl.loop(0, parts * planes // group)
    def _(step):
        pairs = []
        for k in range(group):
            part, plane = step * (group // planes) + k // planes, k % planes
            orbital = orbital_ref[part, plane].astype(F32)
            for s in range(2):
                pair = source_ref[part, s, plane].astype(F32) * orbital
                pairs += [pair.astype(BF16), blank]
        rows = [jnp.concatenate(pairs[4 * k : 4 * k + 4], axis=1) for k in range(group)]
        along_z = dot(jnp.concatenate(rows, axis=0), double_ref[...]).astype(BF16)
        for k in range(group):
            section = dot(table, along_z[k * length : (k + 1) * length])
            at = pl.multiple_of((step * group + k) * PITCH, 8)
            for s in range(2):
                first[s, pl.ds(at, length), :] = section[:, halves[s]]

    @pl.loop(0, length // middle_group)
    def _(step):
        for k in range(middle_group):
            row = step * middle_group + k
            values = [first[s, pl.ds(row, length, stride=PITCH), :].astype(BF16) for s in range(2)]
            section = dot(table, jnp.concatenate(values, axis=1))
            field = field_ref[row]
            values = [(section[:, halves[s]] * field).astype(BF16) for s in range(2)]
            section = dot(table, jnp.concatenate(values, axis=1))
            at = pl.multiple_of(row * PITCH, 8)
            for s in range(2):
                second[s, pl.ds(at, length), :] = section[:, halves[s]]

    @pl.loop(0, parts * planes // group)
    def _(step):
        sections = []
        for k in range(group):
            row = step * group + k
            values = [second[s, pl.ds(row, length, stride=PITCH), :].astype(BF16) for s in range(2)]
            sections.append(dot(table, jnp.concatenate(values, axis=1)).astype(BF16))
        potential = dot(jnp.concatenate(sections, axis=0), double_ref[...])
        for k in range(group):
            part, plane = step * (group // planes) + k // planes, k % planes
            here = potential[k * length : (k + 1) * length]
            terms = [source_ref[part, s, plane].astype(F32) * here[:, halves[s]][:, :width] for s in range(2)]
            total[step * group + k] += terms[0] + terms[1]

    @pl.when(grid_step == pl.num_programs(0) - 1)
    def _():
        @pl.loop(0, parts)
        def _(part):
            for plane in range(planes):
                out_ref[part, plane] = (-EXCHANGE_FRACTION * total[part * planes + plane]).astype(BF16)


def solve(orbital, gathered, field, table, rounds):
    parts, planes, length, width = orbital.shape
    once = pl.Buffered(1)
    return pl.pallas_call(
        solve_kernel,
        grid=(rounds,),
        in_specs=[
            pl.BlockSpec(orbital.shape, lambda r: (0, 0, 0, 0), pipeline_mode=once),
            pl.BlockSpec((parts, 2, planes, length, width), lambda r: (0, r, 0, 0, 0)),
            pl.BlockSpec(field.shape, lambda r: (0, 0, 0), pipeline_mode=once),
            pl.BlockSpec((length, length), lambda r: (0, 0)),
            pl.BlockSpec((2 * LANES, 2 * LANES), lambda r: (0, 0)),
        ],
        out_specs=pl.BlockSpec(orbital.shape, lambda r: (0, 0, 0, 0)),
        out_shape=jax.ShapeDtypeStruct(orbital.shape, BF16),
        scratch_shapes=[
            pltpu.VMEM((2, length * PITCH, LANES), F32),
            pltpu.VMEM((2, length * PITCH, LANES), F32),
            pltpu.VMEM((length, length, width), F32),
        ],
        compiler_params=pltpu.CompilerParams(vmem_limit_bytes=VMEM_LIMIT),
        name="solve",
    )(orbital, gathered, field, table, double_table(table))


def band_sources(orbitals, owners, chosen):
    bands = lax.axis_size("band")
    me = lax.axis_index("band")
    own_round = jnp.argmax(owners == me)
    own = jnp.take(orbitals, chosen[own_round], axis=0)
    shifted = [own]
    for shift in range(1, bands):
        shifted.append(lax.ppermute(own, "band", [(b, (b + shift) % bands) for b in range(bands)]))
    shifted = jnp.stack(shifted)
    return jnp.take(shifted, (me - owners) % bands, axis=0)


def on_device(orbitals, owners, chosen, shell_index, shell_kernel):
    rounds, sources = chosen.shape
    count, planes, length, width = orbitals.shape
    table = cas_table(length)
    slabs = band_sources(orbitals, owners, chosen).reshape(rounds * sources, planes, length, width)
    levels = jnp.swapaxes(shell_index, 0, 1).astype(BF16)
    slabs = jnp.concatenate([slabs, levels[None]], axis=0)
    gathered = lax.all_gather(slabs, "pw")
    orbital = lax.all_to_all(orbitals, "pw", 0, 0, tiled=True)
    field = kernel_field(gathered, shell_kernel)
    applied = solve(orbital, gathered, field, table, rounds)
    return lax.all_to_all(applied, "pw", 0, 0, tiled=True)


def solution(mesh):
    return jax.shard_map(
        on_device,
        mesh=mesh,
        in_specs=(P("band", "pw", None, None), P(), P(), P(None, "pw", None), P()),
        out_specs=P("band", "pw", None, None),
        check_vma=False,
    )
```

```python
import functools
import itertools
import math

import jax
import jax.numpy as jnp
from jax import lax
from jax.experimental import pallas as pl
from jax.experimental.pallas import tpu as pltpu
from jax.sharding import PartitionSpec as P

F32 = jnp.float32
BF16 = jnp.bfloat16
EXCHANGE_FRACTION = 0.25
LANES = 128
ROWS = 16
VMEM_LIMIT = 60 * 2**20
PITCH = 104
BOTH = ("band", "pw")


def cas_table(length):
    counter = lax.iota(jnp.int32, length)
    product = counter[:, None] * counter[None, :] % length
    angles = product.astype(F32) * (2.0 * math.pi / length)
    return ((jnp.cos(angles) + jnp.sin(angles)) / math.sqrt(length)).astype(BF16)


def double_table(table):
    length = table.shape[0]
    wide = jnp.zeros((2 * LANES, 2 * LANES), table.dtype)
    wide = wide.at[:length, :length].set(table)
    return wide.at[LANES : LANES + length, LANES : LANES + length].set(table)


def dot(a, b):
    return jnp.dot(a, b, preferred_element_type=F32)


def pack_tiles(tiles):
    count, width = tiles.shape[-3], tiles.shape[-1]
    free = LANES - width
    kept = count * width // LANES + 1
    thirds = [tiles[..., kept + k // 3, :, (k % 3) * free : (k % 3 + 1) * free] for k in range(3 * (count - kept))]
    thirds += [jnp.zeros_like(thirds[0])] * (kept - len(thirds))
    return jnp.concatenate([tiles[..., :kept, :, :], jnp.stack(thirds, axis=-3)], axis=-1)


def lookup_kernel(level_ref, values_ref, field_ref):
    parts, planes, length, width = level_ref.shape
    values = jnp.broadcast_to(values_ref[...], (length, LANES))
    blank = jnp.zeros((length, LANES - width), jnp.int32)

    @pl.loop(0, parts // 4)
    def _(step):
        for k in range(4):
            part = step * 4 + k
            for plane in range(planes):
                levels = level_ref[part, plane].astype(F32).astype(jnp.int32)
                levels = jnp.concatenate([levels, blank], axis=1)
                field_ref[part * planes + plane] = jnp.take_along_axis(values, levels, axis=1, mode="promise_in_bounds")


def kernel_field(levels, shell_kernel):
    parts, planes, length, width = levels.shape
    return pl.pallas_call(
        lookup_kernel,
        out_shape=jax.ShapeDtypeStruct((parts * planes, length, LANES), F32),
        compiler_params=pltpu.CompilerParams(vmem_limit_bytes=VMEM_LIMIT),
        name="kernel_field",
    )(levels, shell_kernel.reshape(1, LANES))


def unpack_sources(place_ref, pieces, source):
    planes = 3
    length = source.shape[1]
    parts = length // planes
    width = length
    blank = jnp.zeros((length // 2, LANES - width), BF16)
    lows = [pl.multiple_of(h * (length // 2), ROWS) for h in (place_ref[1], 1 - place_ref[1])]
    unroll = 4

    @pl.loop(0, parts // unroll)
    def _(step):
        for k in range(unroll):
            part = step * unroll + k
            for number, ref in enumerate(pieces):
                tiles = [ref[part, t] for t in range(7)]
                spare = [jnp.concatenate([tiles[3 * i + k][:, width:] for k in range(3)], axis=1) for i in range(2)]
                rows = [t[:, :width] for t in tiles] + spare
                for plane in range(planes):
                    here = jnp.concatenate(rows[3 * plane : 3 * plane + 3], axis=0)
                    here = jnp.concatenate([here, blank], axis=1)
                    source[number // 2, part * planes + plane, pl.ds(lows[number % 2], length // 2), :] = here


def solve_kernel(unpack, last, place_ref, near_ref, far_ref, *refs):
    if unpack:
        pieces, refs = refs[:4], refs[4:]
    else:
        source, refs = refs[0], refs[1:]
    field_hbm, table_ref, double_ref = refs[:3]
    refs = refs[3:]
    if last:
        before_hbm, keep_ref, send_ref = refs[:3]
        refs = refs[3:]
    else:
        total_ref, refs = refs[0], refs[1:]
    if unpack:
        source, refs = refs[0], refs[1:]
    first, second, field = refs[:3]
    refs = refs[3:]
    semaphores = refs[-1]
    chips, planes, length, width = near_ref.shape
    chip_group = 4
    table = table_ref[...]
    halves = (slice(0, LANES), slice(LANES, 2 * LANES))
    blank = jnp.zeros((length, LANES - width), BF16)
    field_copy = pltpu.make_async_copy(field_hbm, field, semaphores.at[0])
    field_copy.start()
    if last:
        before = refs[0]
        before_copy = pltpu.make_async_copy(before_hbm, before, semaphores.at[1])
        before_copy.start()
    if unpack:
        unpack_sources(place_ref, pieces, source)
    core = place_ref[0]

    def sections_of(step):
        for k in range(chip_group):
            chip = step * chip_group + k
            for near in (True, False):
                for plane in range(planes):
                    yield chip, near, plane, (2 * chip + (core if near else 1 - core)) * planes + plane

    @pl.loop(0, chips // chip_group)
    def _(step):
        rows = []
        for chip, near, plane, row in sections_of(step):
            orbital = (near_ref if near else far_ref)[chip, plane]
            orbital = jnp.concatenate([orbital, blank], axis=1).astype(F32)
            pair = [(source[s, row].astype(F32) * orbital).astype(BF16) for s in range(2)]
            rows.append(jnp.concatenate(pair, axis=1))
        along_z = dot(jnp.concatenate(rows, axis=0), double_ref[...]).astype(BF16)
        for k, (chip, near, plane, row) in enumerate(sections_of(step)):
            section = dot(table, along_z[k * length : (k + 1) * length])
            at = pl.multiple_of(row * PITCH, 8)
            for s in range(2):
                first[s, pl.ds(at, length), :] = section[:, halves[s]]

    field_copy.wait()
    group = 24

    @pl.loop(0, length // group)
    def _(step):
        for k in range(group):
            row = step * group + k
            values = [first[s, pl.ds(row, length, stride=PITCH), :].astype(BF16) for s in range(2)]
            section = dot(table, jnp.concatenate(values, axis=1))
            values = [(section[:, halves[s]] * field[row]).astype(BF16) for s in range(2)]
            section = dot(table, jnp.concatenate(values, axis=1))
            at = pl.multiple_of(row * PITCH, 8)
            for s in range(2):
                second[s, pl.ds(at, length), :] = section[:, halves[s]]

    if last:
        before_copy.wait()

    @pl.loop(0, chips // chip_group)
    def _(step):
        sections = []
        for chip, near, plane, row in sections_of(step):
            values = [second[s, pl.ds(row, length, stride=PITCH), :].astype(BF16) for s in range(2)]
            sections.append(dot(table, jnp.concatenate(values, axis=1)).astype(BF16))
        potential = dot(jnp.concatenate(sections, axis=0), double_ref[...])
        for k, (chip, near, plane, row) in enumerate(sections_of(step)):
            here = potential[k * length : (k + 1) * length]
            terms = [source[s, row].astype(F32) * here[:, halves[s]] for s in range(2)]
            result = terms[0] + terms[1]
            if last:
                result = (-EXCHANGE_FRACTION * (result + before[row]))[:, :width]
                if near:
                    keep_ref[chip, plane] = result
                else:
                    send_ref[chip, plane] = result.astype(BF16)
            else:
                total_ref[row] = result


def solve(place, orbital, pieces, source, field, table, before):
    near, far = orbital
    length = near.shape[2]
    whole = (length, length, LANES)
    vmem = pl.BlockSpec(memory_space=pltpu.VMEM)
    hbm = pl.BlockSpec(memory_space=pl.ANY)
    unpack, last = source is None, before is not None
    given = list(pieces) if unpack else [source]
    operands = [place, near, far, *given, field, table, double_table(table)]
    in_specs = [pl.BlockSpec(memory_space=pltpu.SMEM), vmem, vmem] + [vmem] * len(given) + [hbm, vmem, vmem]
    scratch = [pltpu.VMEM((2, length * PITCH, LANES), F32)] * 2 + [pltpu.VMEM(whole, F32)]
    if last:
        operands.append(before)
        in_specs.append(hbm)
        scratch.append(pltpu.VMEM(whole, F32))
        out = [jax.ShapeDtypeStruct(near.shape, F32), jax.ShapeDtypeStruct(near.shape, BF16)]
    else:
        out = [jax.ShapeDtypeStruct(whole, F32)]
    if unpack:
        out.append(jax.ShapeDtypeStruct((2,) + whole, BF16))
    return pl.pallas_call(
        functools.partial(solve_kernel, unpack, last),
        in_specs=in_specs,
        out_specs=[vmem] * len(out),
        out_shape=out,
        scratch_shapes=scratch + [pltpu.SemaphoreType.DMA((2,))],
        compiler_params=pltpu.CompilerParams(vmem_limit_bytes=VMEM_LIMIT),
        cost_estimate=pl.CostEstimate(flops=24 * length**4 * 6, bytes_accessed=8 * length**3, transcendentals=0),
        name="solve",
    )(*operands)


def device(y, x, z, core):
    return ((y * 2 + x // 2) * 2 + x % 2) * 16 + z * 2 + core


def shift(value, dy=0, dx=0, dz=0, core=0):
    places = itertools.product(range(4), range(4), range(8), range(2))
    pairs = [
        (device(y, x, z, c), device((y + dy) % 4, (x + dx) % 4, (z + dz) % 8, c ^ core)) for y, x, z, c in places
    ]
    return lax.ppermute(value, BOTH, pairs)


def chip_groups(bands, parts):
    return [[b * parts + 2 * p + c for p in range(parts // 2)] for b in range(bands) for c in range(2)]


def between_chips(value):
    groups = chip_groups(lax.axis_size("band"), lax.axis_size("pw"))
    return lax.all_to_all(value, BOTH, 0, 0, axis_index_groups=groups, tiled=True)


def own_pieces(orbitals, owners, chosen):
    me = lax.axis_index("band")
    planes, length, width = orbitals.shape[1:]
    own_round = jnp.argmax(owners == me)
    own = jnp.take(orbitals, chosen[own_round], axis=0)
    tiles = own.reshape(2, planes, 2, length // 2 // ROWS, ROWS, width)
    tiles = tiles.transpose(2, 0, 1, 3, 4, 5).reshape(2, 2, planes * length // 2 // ROWS, ROWS, width)
    packed = pack_tiles(tiles)
    received = lax.all_to_all(jnp.concatenate([packed] * 4, axis=0), "band", 0, 0, tiled=True)
    return lax.dynamic_index_in_dim(received, owners[me // 2], 0, keepdims=False)


def on_device(orbitals, owners, chosen, shell_index, shell_kernel):
    band, part = lax.axis_index("band"), lax.axis_index("pw")
    count, planes, length, width = orbitals.shape
    table = cas_table(length)
    place = jnp.stack([part % 2, band % 2])
    levels = lax.all_gather(jnp.swapaxes(shell_index, 0, 1).astype(BF16), "pw")
    by_core = orbitals.reshape(count // 2, 2, planes, length, width)

    pieces = own_pieces(orbitals, owners, chosen)
    copies = jnp.broadcast_to(pieces[None], (count // 2,) + pieces.shape).reshape((count,) + pieces.shape[1:])
    own = lax.all_to_all(copies, "pw", 0, 0, tiled=True)
    across = shift(own, dx=2)
    opposite = shift(own, dy=2)
    both = jnp.stack([own, across])
    beside = [shift(both, dy=dy) for dy in (1, 3)]
    pairs = [[own, across, opposite, shift(opposite, dx=2)]]
    pairs.append([beside[k][h] for k in range(2) for h in range(2)])
    second_half, across, opposite = lax.optimization_barrier((by_core[:, 1], across, opposite))
    halves = [by_core[:, 0], second_half]

    field = kernel_field(levels, shell_kernel)
    unpacked = [None, None]
    applied = []
    for which in range(2):
        near = between_chips(halves[which])
        orbital = (near, shift(near, core=1))
        total, *given = solve(place, orbital, pairs[0], unpacked[0], field, table, None)
        if which == 0:
            unpacked[0] = given[0]
        keep, send, *given = solve(place, orbital, pairs[1], unpacked[1], field, table, total)
        if which == 0:
            unpacked[1] = given[0]
            unpacked[0], send = lax.optimization_barrier((unpacked[0], send))
        result = (keep + shift(send, core=1).astype(F32)).astype(BF16)
        applied.append(between_chips(result))
    return jnp.stack(applied, axis=1).reshape(orbitals.shape)


def solution(mesh):
    return jax.shard_map(
        on_device,
        mesh=mesh,
        in_specs=(P("band", "pw", None, None), P(), P(), P(None, "pw", None), P()),
        out_specs=P("band", "pw", None, None),
        check_vma=False,
    )
```

```python
import functools
import itertools
import math

import jax
import jax.numpy as jnp
import ml_dtypes
import numpy as np
from jax import lax
from jax.experimental import pallas as pl
from jax.experimental.pallas import tpu as pltpu
from jax.sharding import PartitionSpec as P

F32 = jnp.float32
BF16 = jnp.bfloat16
EXCHANGE_FRACTION = 0.25
LANES = 128
ROWS = 16
SLAB = 14
PIECE = 7
VMEM_LIMIT = 60 * 2**20
PITCH = 104
CHIP_GROUP = 8
BOTH = ("band", "pw")
HALVES = (slice(0, LANES), slice(LANES, 2 * LANES))


def cas_table(length):
    counter = np.arange(length)
    angles = counter[:, None] * counter[None, :] % length * (2.0 * math.pi / length)
    return ((np.cos(angles) + np.sin(angles)) / math.sqrt(length)).astype(ml_dtypes.bfloat16)


def double_table(table):
    length = table.shape[0]
    wide = np.zeros((2 * LANES, 2 * LANES), table.dtype)
    for low in (0, LANES):
        wide[low : low + length, low : low + length] = table
    return wide


def dot(a, b):
    return jnp.dot(a, b, preferred_element_type=F32)


def pack_tiles(tiles, kept):
    count, width = tiles.shape[-3], tiles.shape[-1]
    free = LANES - width
    thirds = [tiles[..., kept + k // 3, :, (k % 3) * free : (k % 3 + 1) * free] for k in range(3 * (count - kept))]
    thirds += [jnp.zeros_like(thirds[0])] * (kept - len(thirds))
    return jnp.concatenate([tiles[..., :kept, :, :], jnp.stack(thirds, axis=-3)], axis=-1)


def packed_rows(rows):
    width = rows[0].shape[1]
    free = LANES - width
    last = len(rows) - SLAB
    thirds = [rows[SLAB + k // 3][:, (k % 3) * free : (k % 3 + 1) * free] for k in range(3 * last)]
    thirds += [jnp.zeros_like(thirds[0])] * (SLAB - len(thirds))
    return [jnp.concatenate([rows[t], thirds[t]], axis=1) for t in range(SLAB)]


def unpacked_rows(tiles, count, width):
    extra = count - len(tiles)
    spare = [jnp.concatenate([tiles[3 * j + k][:, width:] for k in range(3)], axis=1) for j in range(extra)]
    return [t[:, :width] for t in tiles] + spare


def slab_planes(ref, chip, low, planes, length):
    per_plane = length // ROWS
    rows = unpacked_rows([ref[chip, low + t] for t in range(SLAB)], planes * per_plane, length)
    return [jnp.concatenate(rows[p * per_plane : (p + 1) * per_plane], axis=0) for p in range(planes)]


def slab_tiles(planes):
    return [plane[t * ROWS : (t + 1) * ROWS] for plane in planes for t in range(plane.shape[0] // ROWS)]


def pack_kernel(orbital_ref, index_ref, values_ref, even_ref, odd_ref):
    planes, length, width = index_ref.shape
    values = jnp.broadcast_to(values_ref[...], (length, LANES))
    blank = jnp.zeros((length, LANES - width), jnp.int32)
    field = []
    for plane in range(planes):
        levels = jnp.concatenate([index_ref[plane], blank], axis=1)
        here = jnp.take_along_axis(values, levels, axis=1, mode="promise_in_bounds")
        field.append(here[:, :width].astype(BF16))
    field = packed_rows(slab_tiles(field))
    chips = even_ref.shape[0]
    unroll = 4

    @pl.loop(0, chips // unroll)
    def _(step):
        for k in range(unroll):
            chip = step * unroll + k
            for which, ref in enumerate((even_ref, odd_ref)):
                slab = [orbital_ref[2 * chip + which, p] for p in range(planes)]
                for t, tile in enumerate(packed_rows(slab_tiles(slab))):
                    ref[chip, t] = tile
            for t in range(SLAB):
                even_ref[chip, SLAB + t] = field[t]


def pack_slabs(orbitals, shell_index, shell_kernel):
    chips = orbitals.shape[0] // 2
    vmem = pl.BlockSpec(memory_space=pltpu.VMEM)
    return pl.pallas_call(
        pack_kernel,
        in_specs=[vmem] * 3,
        out_specs=[vmem] * 2,
        out_shape=[jax.ShapeDtypeStruct((chips, n * SLAB, ROWS, LANES), BF16) for n in (2, 1)],
        compiler_params=pltpu.CompilerParams(vmem_limit_bytes=VMEM_LIMIT),
        name="pack",
    )(orbitals, shell_index, shell_kernel.reshape(1, LANES))


def unpack_sources(place_ref, pieces, planes, source):
    length = source.shape[1]
    per_plane = length // 2 // ROWS
    blank = jnp.zeros((length // 2, LANES - length), BF16)
    lows = [pl.multiple_of(h * (length // 2), ROWS) for h in (place_ref[1], 1 - place_ref[1])]
    unroll = 8

    @pl.loop(0, length // planes // unroll)
    def _(step):
        for k in range(unroll):
            part = step * unroll + k
            for number, ref in enumerate(pieces):
                rows = unpacked_rows([ref[part, t] for t in range(PIECE)], planes * per_plane, length)
                for plane in range(planes):
                    here = jnp.concatenate(rows[per_plane * plane : per_plane * (plane + 1)], axis=0)
                    here = jnp.concatenate([here, blank], axis=1)
                    source[number // 2, part * planes + plane, pl.ds(lows[number % 2], length // 2), :] = here


def solve_pair(core, planes, orbital, source, fields, tables, scratch, finish):
    near_ref, far_ref = orbital
    table_ref, double_ref = tables
    first, second = scratch
    chips = near_ref.shape[0]
    length = table_ref.shape[0]
    table = table_ref[...]
    blank = jnp.zeros((length, LANES - length), BF16)

    def slabs_of(step):
        for k in range(CHIP_GROUP):
            for near in (True, False):
                chip = step * CHIP_GROUP + k
                yield chip, near, (2 * chip + (core if near else 1 - core)) * planes

    @pl.loop(0, chips // CHIP_GROUP)
    def _(step):
        rows = []
        for chip, near, base in slabs_of(step):
            for p, plane in enumerate(slab_planes(near_ref if near else far_ref, chip, 0, planes, length)):
                plane = jnp.concatenate([plane, blank], axis=1).astype(F32)
                pair = [(source[s, base + p].astype(F32) * plane).astype(BF16) for s in range(2)]
                rows.append(jnp.concatenate(pair, axis=1))
        along_z = dot(jnp.concatenate(rows, axis=0), double_ref[...]).astype(BF16)
        for k, (chip, near, base) in enumerate(slabs_of(step)):
            for p in range(planes):
                low = (k * planes + p) * length
                section = dot(table, along_z[low : low + length])
                at = pl.multiple_of((base + p) * PITCH, 8)
                for s in range(2):
                    first[s, pl.ds(at, length), :] = section[:, HALVES[s]]

    @pl.loop(0, chips // CHIP_GROUP)
    def _(step):
        for chip, near, base in slabs_of(step):
            for p, field in enumerate(slab_planes(fields[0] if near else fields[1], chip, SLAB, planes, length)):
                field = jnp.concatenate([field, blank], axis=1).astype(F32)
                row = base + p
                values = [first[s, pl.ds(row, length, stride=PITCH), :].astype(BF16) for s in range(2)]
                section = dot(table, jnp.concatenate(values, axis=1))
                values = [(section[:, HALVES[s]] * field).astype(BF16) for s in range(2)]
                section = dot(table, jnp.concatenate(values, axis=1))
                at = pl.multiple_of(row * PITCH, 8)
                for s in range(2):
                    second[s, pl.ds(at, length), :] = section[:, HALVES[s]]

    @pl.loop(0, chips // CHIP_GROUP)
    def _(step):
        sections = []
        for chip, near, base in slabs_of(step):
            for p in range(planes):
                values = [second[s, pl.ds(base + p, length, stride=PITCH), :].astype(BF16) for s in range(2)]
                sections.append(dot(table, jnp.concatenate(values, axis=1)).astype(BF16))
        potential = dot(jnp.concatenate(sections, axis=0), double_ref[...])
        for k, (chip, near, base) in enumerate(slabs_of(step)):
            terms = []
            for p in range(planes):
                low = (k * planes + p) * length
                here = potential[low : low + length]
                both = [source[s, base + p].astype(F32) * here[:, HALVES[s]] for s in range(2)]
                terms.append(both[0] + both[1])
            finish(chip, near, base, terms)


def store_scaled(chip, near, sums, keep_ref, send_ref):
    length = sums[0].shape[0]
    rows = slab_tiles([(-EXCHANGE_FRACTION * value)[:, :length] for value in sums])
    for t, tile in enumerate(packed_rows(rows)):
        if near:
            keep_ref[chip, t] = tile
        else:
            send_ref[chip, t] = tile.astype(BF16)


def first_kernel(last, planes, place_ref, near_ref, far_ref, *refs):
    pieces, refs = refs[:4], refs[4:]
    table_ref, double_ref = refs[:2]
    refs = refs[2:]
    if last:
        before_hbm, keep_ref, send_ref, source, first, second, before, semaphore = refs
        before_copy = pltpu.make_async_copy(before_hbm, before, semaphore)
        before_copy.start()
    else:
        total_ref, source, first, second = refs
    unpack_sources(place_ref, pieces, planes, source)
    if last:
        before_copy.wait()

    def finish(chip, near, base, terms):
        if last:
            sums = [before[base + p] + terms[p] for p in range(planes)]
            store_scaled(chip, near, sums, keep_ref, send_ref)
        else:
            for p in range(planes):
                total_ref[base + p] = terms[p]

    orbital = (near_ref, far_ref)
    solve_pair(place_ref[0], planes, orbital, source, orbital, (table_ref, double_ref), (first, second), finish)


def second_kernel(planes, place_ref, near_ref, far_ref, near_field, far_field, one_hbm, two_hbm, table_ref, double_ref,
                  keep_ref, send_ref, sources, first, second, total, semaphores):
    copies = [
        pltpu.make_async_copy(ref, sources.at[k], semaphores.at[k]) for k, ref in enumerate((one_hbm, two_hbm))
    ]
    for copy in copies:
        copy.start()
    copies[0].wait()

    def keep_total(chip, near, base, terms):
        for p in range(planes):
            total[base + p] = terms[p]

    def finish(chip, near, base, terms):
        store_scaled(chip, near, [total[base + p] + terms[p] for p in range(planes)], keep_ref, send_ref)

    orbital, fields = (near_ref, far_ref), (near_field, far_field)
    tables, scratch = (table_ref, double_ref), (first, second)
    core = place_ref[0]
    solve_pair(core, planes, orbital, sources.at[0], fields, tables, scratch, keep_total)
    copies[1].wait()
    solve_pair(core, planes, orbital, sources.at[1], fields, tables, scratch, finish)


def solve_call(kernel, operands, in_hbm, outs, scratch, length, pairs):
    vmem = pl.BlockSpec(memory_space=pltpu.VMEM)
    specs = [pl.BlockSpec(memory_space=pl.ANY) if k in in_hbm else vmem for k in range(len(operands))]
    specs[0] = pl.BlockSpec(memory_space=pltpu.SMEM)
    return pl.pallas_call(
        kernel,
        in_specs=specs,
        out_specs=[vmem] * len(outs),
        out_shape=outs,
        scratch_shapes=scratch,
        compiler_params=pltpu.CompilerParams(vmem_limit_bytes=VMEM_LIMIT),
        cost_estimate=pl.CostEstimate(
            flops=144 * length**4 * pairs, bytes_accessed=8 * length**3, transcendentals=0
        ),
        name="solve",
    )(*operands)


def solve_first(place, orbital, pieces, table, before, planes):
    near, far = orbital
    length = table.shape[0]
    whole = (length, length, LANES)
    last = before is not None
    operands = [place, near, far, *pieces, table, double_table(table)]
    in_hbm = []
    section = pltpu.VMEM((2, (length + 1) * PITCH, LANES), F32)
    scratch = [section, section]
    if last:
        in_hbm.append(len(operands))
        operands.append(before)
        scratch += [pltpu.VMEM(whole, F32), pltpu.SemaphoreType.DMA]
        slab = (near.shape[0], SLAB) + near.shape[2:]
        outs = [jax.ShapeDtypeStruct(slab, F32), jax.ShapeDtypeStruct(slab, BF16)]
    else:
        outs = [jax.ShapeDtypeStruct(whole, F32)]
    outs.append(jax.ShapeDtypeStruct((2,) + whole, BF16))
    return solve_call(functools.partial(first_kernel, last, planes), operands, in_hbm, outs, scratch, length, 1)


def solve_second(place, orbital, field, sources, table, planes):
    near, far = orbital
    length = table.shape[0]
    whole = (length, length, LANES)
    section = pltpu.VMEM((2, (length + 1) * PITCH, LANES), F32)
    outs = [jax.ShapeDtypeStruct(near.shape, F32), jax.ShapeDtypeStruct(near.shape, BF16)]
    scratch = [pltpu.VMEM((2, 2) + whole, BF16), section, section, pltpu.VMEM(whole, F32)]
    scratch.append(pltpu.SemaphoreType.DMA((2,)))
    operands = [place, near, far, *field, *sources, table, double_table(table)]
    return solve_call(functools.partial(second_kernel, planes), operands, (5, 6), outs, scratch, length, 2)


def unpack_kernel(slab_ref, *refs):
    out_ref = refs[-1]
    planes, length = out_ref.shape[2:4]
    for chip in range(slab_ref.shape[0]):
        for p, plane in enumerate(slab_planes(slab_ref, chip, 0, planes, length)):
            out_ref[chip, 0, p] = plane


def unpack_slabs(slabs, which, before, planes, length):
    chips = slabs.shape[0]
    steps = 2
    block = pl.BlockSpec((chips // steps,) + slabs.shape[1:], lambda i: (i, 0, 0, 0))
    given = [] if before is None else [before]
    return pl.pallas_call(
        unpack_kernel,
        grid=(steps,),
        in_specs=[block] + [pl.BlockSpec(memory_space=pl.ANY)] * len(given),
        out_specs=pl.BlockSpec((chips // steps, 1, planes, length, length), lambda i: (i, which, 0, 0, 0)),
        out_shape=jax.ShapeDtypeStruct((chips, 2, planes, length, length), BF16),
        input_output_aliases={1: 0} if given else {},
        compiler_params=pltpu.CompilerParams(vmem_limit_bytes=VMEM_LIMIT),
        name="unpack",
    )(slabs, *given)


def device(y, x, z, core):
    return ((y * 2 + x // 2) * 2 + x % 2) * 16 + z * 2 + core


def moved(value, dy=0, mirror=False, core=0):
    places = itertools.product(range(4), range(4), range(8), range(2))
    pairs = [(device(y, x, z, c), device((y + dy) % 4, 3 - x if mirror else x, z, c ^ core)) for y, x, z, c in places]
    return lax.ppermute(value, BOTH, pairs)


def between_chips(value):
    bands, parts = lax.axis_size("band"), lax.axis_size("pw")
    groups = [[b * parts + 2 * p + c for p in range(parts // 2)] for b in range(bands) for c in range(2)]
    return lax.all_to_all(value, BOTH, 0, 0, axis_index_groups=groups, tiled=True)


def own_pieces(orbitals, owners, chosen):
    me = lax.axis_index("band")
    planes, length, width = orbitals.shape[1:]
    rows = jnp.sum(jnp.where((owners == me)[:, None], chosen, 0), axis=0)
    own = jnp.concatenate([lax.dynamic_slice_in_dim(orbitals, rows[s], 1) for s in range(2)], axis=0)
    tiles = own.reshape(2, planes, 2, length // 2 // ROWS, ROWS, width)
    tiles = tiles.transpose(2, 0, 1, 3, 4, 5).reshape(2, 2, planes * length // 2 // ROWS, ROWS, width)
    packed = pack_tiles(tiles, PIECE)
    received = lax.all_to_all(jnp.concatenate([packed] * 4, axis=0), "band", 0, 0, tiled=True)
    return lax.dynamic_index_in_dim(received, owners[me // 2], 0, keepdims=False)


def on_device(orbitals, owners, chosen, shell_index, shell_kernel):
    band, part = lax.axis_index("band"), lax.axis_index("pw")
    count, planes, length, width = orbitals.shape
    table = cas_table(length)
    place = jnp.stack([part % 2, band % 2])

    pieces = own_pieces(orbitals, owners, chosen)
    copies = jnp.broadcast_to(pieces[None], (count // 2,) + pieces.shape).reshape((count,) + pieces.shape[1:])
    own = lax.all_to_all(copies, "pw", 0, 0, tiled=True)
    across = moved(own, mirror=True)
    opposite = moved(own, dy=2)
    opposite_across = moved(opposite, mirror=True)
    later_own, _ = lax.optimization_barrier((own, opposite))
    beside = [moved(later_own, dy=dy) for dy in (1, 3)]

    slabs = list(pack_slabs(orbitals, jnp.swapaxes(shell_index, 0, 1), shell_kernel))
    even = between_chips(slabs[0])
    even, across, opposite_across, *beside = lax.optimization_barrier((even, across, opposite_across, *beside))
    beside_across = [moved(across, dy=dy) for dy in (1, 3)]
    even = (even, moved(even, core=1))
    slabs[1], _ = lax.optimization_barrier((slabs[1], across))
    odd = between_chips(slabs[1])
    odd = (odd, moved(odd, core=1))

    def finished(keep, send):
        return between_chips((keep + moved(send, core=1).astype(F32)).astype(BF16))

    pieces = [own, across, opposite, opposite_across]
    total, one = solve_first(place, even, pieces, table, None, planes)
    pieces = [beside[0], beside_across[0], beside[1], beside_across[1]]
    keep, send, two = solve_first(place, even, pieces, table, total, planes)
    result = unpack_slabs(finished(keep, send), 0, None, planes, length)
    keep, send = solve_second(place, odd, even, (one, two), table, planes)
    result = unpack_slabs(finished(keep, send), 1, result, planes, length)
    return result.reshape(orbitals.shape)


def solution(mesh):
    return jax.shard_map(
        on_device,
        mesh=mesh,
        in_specs=(P("band", "pw", None, None), P(), P(), P(None, "pw", None), P()),
        out_specs=P("band", "pw", None, None),
        check_vma=False,
    )
```

```python
import functools
import itertools
import math

import jax
import jax.numpy as jnp
import ml_dtypes
import numpy as np
from jax import lax
from jax.experimental import pallas as pl
from jax.experimental.pallas import tpu as pltpu
from jax.sharding import PartitionSpec as P

F32 = jnp.float32
BF16 = jnp.bfloat16
EXCHANGE_FRACTION = 0.25
LANES = 128
ROWS = 16
SLAB = 14
PIECE = 7
VMEM_LIMIT = 60 * 2**20
PITCH = 104
CHIP_GROUP = 8
BOTH = ("band", "pw")
HALVES = (slice(0, LANES), slice(LANES, 2 * LANES))


def cas_table(length):
    counter = np.arange(length)
    angles = counter[:, None] * counter[None, :] % length * (2.0 * math.pi / length)
    return ((np.cos(angles) + np.sin(angles)) / math.sqrt(length)).astype(ml_dtypes.bfloat16)


def double_table(table):
    length = table.shape[0]
    wide = np.zeros((2 * LANES, 2 * LANES), table.dtype)
    for low in (0, LANES):
        wide[low : low + length, low : low + length] = table
    return wide


def dot(a, b):
    return jnp.dot(a, b, preferred_element_type=F32)


def packed_rows(rows, kept):
    width = rows[0].shape[1]
    free = LANES - width
    thirds = [rows[kept + k // 3][:, (k % 3) * free : (k % 3 + 1) * free] for k in range(3 * (len(rows) - kept))]
    thirds += [jnp.zeros_like(thirds[0])] * (kept - len(thirds))
    return [jnp.concatenate([rows[t], thirds[t]], axis=1) for t in range(kept)]


def unpacked_rows(tiles, count, width):
    extra = count - len(tiles)
    spare = [jnp.concatenate([tiles[3 * j + k][:, width:] for k in range(3)], axis=1) for j in range(extra)]
    return [t[:, :width] for t in tiles] + spare


def slab_planes(ref, chip, planes, length):
    per_plane = length // ROWS
    rows = unpacked_rows([ref[chip, t] for t in range(SLAB)], planes * per_plane, length)
    return [jnp.concatenate(rows[p * per_plane : (p + 1) * per_plane], axis=0) for p in range(planes)]


def slab_tiles(planes):
    return [plane[t * ROWS : (t + 1) * ROWS] for plane in planes for t in range(plane.shape[0] // ROWS)]


def pack_kernel(orbital_ref, index_ref, values_ref, even_ref, odd_ref):
    planes, length, width = index_ref.shape
    values = jnp.broadcast_to(values_ref[...], (length, LANES))
    blank = jnp.zeros((length, LANES - width), jnp.int32)
    field = []
    for plane in range(planes):
        levels = jnp.concatenate([index_ref[plane], blank], axis=1)
        here = jnp.take_along_axis(values, levels, axis=1, mode="promise_in_bounds")
        field.append(here[:, :width].astype(BF16))
    field = packed_rows(slab_tiles(field), SLAB)
    chips = even_ref.shape[0]
    unroll = 4

    @pl.loop(0, chips // unroll)
    def _(step):
        for k in range(unroll):
            chip = step * unroll + k
            for which, ref in enumerate((even_ref, odd_ref)):
                slab = [orbital_ref[2 * chip + which, p] for p in range(planes)]
                for t, tile in enumerate(packed_rows(slab_tiles(slab), SLAB)):
                    ref[chip, t] = tile
            for t in range(SLAB):
                even_ref[chip, SLAB + t] = field[t]


def pack_slabs(orbitals, shell_index, shell_kernel):
    chips = orbitals.shape[0] // 2
    vmem = pl.BlockSpec(memory_space=pltpu.VMEM)
    return pl.pallas_call(
        pack_kernel,
        in_specs=[vmem] * 3,
        out_specs=[vmem] * 2,
        out_shape=[jax.ShapeDtypeStruct((chips, n * SLAB, ROWS, LANES), BF16) for n in (2, 1)],
        compiler_params=pltpu.CompilerParams(vmem_limit_bytes=VMEM_LIMIT),
        name="pack",
    )(orbitals, shell_index, shell_kernel.reshape(1, LANES))


def unpack_sources(place_ref, pieces, planes, source):
    length = source.shape[1]
    per_plane = length // 2 // ROWS
    blank = jnp.zeros((length // 2, LANES - length), BF16)
    lows = [pl.multiple_of(h * (length // 2), ROWS) for h in (place_ref[1], 1 - place_ref[1])]
    unroll = 8

    @pl.loop(0, length // planes // unroll)
    def _(step):
        for k in range(unroll):
            part = step * unroll + k
            for number, ref in enumerate(pieces):
                rows = unpacked_rows([ref[part, t] for t in range(PIECE)], planes * per_plane, length)
                for plane in range(planes):
                    here = jnp.concatenate(rows[per_plane * plane : per_plane * (plane + 1)], axis=0)
                    here = jnp.concatenate([here, blank], axis=1)
                    source[number // 2, part * planes + plane, pl.ds(lows[number % 2], length // 2), :] = here


def solve_pair(core, planes, orbital, source, fields, tables, scratch, wait_fields, finish, step_done):
    near_ref, far_ref = orbital
    table_ref, double_ref = tables
    first, second = scratch
    chips = near_ref.shape[0]
    length = table_ref.shape[0]
    table = table_ref[...]
    blank = jnp.zeros((length, LANES - length), BF16)

    def slabs_of(step):
        for k in range(CHIP_GROUP):
            for near in (True, False):
                chip = step * CHIP_GROUP + k
                yield chip, near, (2 * chip + (core if near else 1 - core)) * planes

    @pl.loop(0, chips // CHIP_GROUP)
    def _(step):
        rows = []
        for chip, near, base in slabs_of(step):
            for p, plane in enumerate(slab_planes(near_ref if near else far_ref, chip, planes, length)):
                plane = jnp.concatenate([plane, blank], axis=1).astype(F32)
                pair = [(source[s, base + p].astype(F32) * plane).astype(BF16) for s in range(2)]
                rows.append(jnp.concatenate(pair, axis=1))
        along_z = dot(jnp.concatenate(rows, axis=0), double_ref[...]).astype(BF16)
        for k, (chip, near, base) in enumerate(slabs_of(step)):
            for p in range(planes):
                low = (k * planes + p) * length
                section = dot(table, along_z[low : low + length])
                at = pl.multiple_of((base + p) * PITCH, 8)
                for s in range(2):
                    first[s, pl.ds(at, length), :] = section[:, HALVES[s]]

    wait_fields()

    @pl.loop(0, chips // CHIP_GROUP)
    def _(step):
        for chip, near, base in slabs_of(step):
            for p, field in enumerate(slab_planes(fields[0] if near else fields[1], chip, planes, length)):
                field = jnp.concatenate([field, blank], axis=1).astype(F32)
                row = base + p
                values = [first[s, pl.ds(row, length, stride=PITCH), :].astype(BF16) for s in range(2)]
                section = dot(table, jnp.concatenate(values, axis=1))
                values = [(section[:, HALVES[s]] * field).astype(BF16) for s in range(2)]
                section = dot(table, jnp.concatenate(values, axis=1))
                at = pl.multiple_of(row * PITCH, 8)
                for s in range(2):
                    second[s, pl.ds(at, length), :] = section[:, HALVES[s]]

    @pl.loop(0, chips // CHIP_GROUP)
    def _(step):
        sections = []
        for chip, near, base in slabs_of(step):
            for p in range(planes):
                values = [second[s, pl.ds(base + p, length, stride=PITCH), :].astype(BF16) for s in range(2)]
                sections.append(dot(table, jnp.concatenate(values, axis=1)).astype(BF16))
        potential = dot(jnp.concatenate(sections, axis=0), double_ref[...])
        for k, (chip, near, base) in enumerate(slabs_of(step)):
            terms = []
            for p in range(planes):
                low = (k * planes + p) * length
                here = potential[low : low + length]
                both = [source[s, base + p].astype(F32) * here[:, HALVES[s]] for s in range(2)]
                terms.append(both[0] + both[1])
            finish(chip, near, base, terms)
        step_done(step)


def store_scaled(chip, near, sums, keep_ref, send_ref):
    length = sums[0].shape[0]
    rows = slab_tiles([(-EXCHANGE_FRACTION * value)[:, :length] for value in sums])
    for t, tile in enumerate(packed_rows(rows, SLAB)):
        if near:
            keep_ref[chip, t] = tile
        else:
            send_ref[chip, t] = tile.astype(BF16)


def started(pairs, semaphores, low):
    copies = [pltpu.make_async_copy(*pair, semaphores.at[low + k]) for k, pair in enumerate(pairs)]
    for copy in copies:
        copy.start()
    return copies


def wait_for(copies):
    for copy in copies:
        copy.wait()


def nothing(*_):
    pass


def first_kernel(last, planes, place_ref, *refs):
    slabs_hbm, pieces_hbm, (table_ref, double_ref), refs = refs[:2], refs[2:6], refs[6:8], refs[8:]
    if last:
        before_hbm, keep_ref, send_ref, *refs = refs
    else:
        total_hbm, *refs = refs
    slabs, pieces, source, first, second, total, semaphores = refs
    piece_copies = started([(ref, pieces.at[k]) for k, ref in enumerate(pieces_hbm)], semaphores, 0)
    slab_copies = started([(ref, slabs.at[k]) for k, ref in enumerate(slabs_hbm)], semaphores, 4)
    if last:
        total_copies = started([(before_hbm, total)], semaphores, 6)
    wait_for(piece_copies)
    unpack_sources(place_ref, [pieces.at[k] for k in range(4)], planes, source)
    wait_for(slab_copies)
    chunk = CHIP_GROUP * 2 * planes

    def rows_out(step):
        rows = pl.ds(pl.multiple_of(step * chunk, chunk), chunk)
        return pltpu.make_async_copy(total.at[rows], total_hbm.at[rows], semaphores.at[6 + step])

    def wait_fields():
        if last:
            wait_for(total_copies)

    def finish(chip, near, base, terms):
        if last:
            sums = [total[base + p] + terms[p] for p in range(planes)]
            store_scaled(chip, near, sums, keep_ref, send_ref)
        else:
            for p in range(planes):
                total[base + p] = terms[p]

    def step_done(step):
        if not last:
            rows_out(step).start()

    orbital = [slabs.at[k, :, 0:SLAB] for k in range(2)]
    fields = [slabs.at[k, :, SLAB : 2 * SLAB] for k in range(2)]
    tables, scratch = (table_ref, double_ref), (first, second)
    solve_pair(place_ref[0], planes, orbital, source, fields, tables, scratch, wait_fields, finish, step_done)
    if not last:
        for step in range(total.shape[0] // chunk):
            rows_out(step).wait()


def second_kernel(planes, place_ref, *refs):
    slabs_hbm, other_hbm, pieces_hbm, (table_ref, double_ref), refs = refs[:2], refs[2:4], refs[4:12], refs[12:14], refs[14:]
    keep_ref, send_ref, slabs, fields, pieces, source, first, second, total, semaphores = refs
    piece_pairs = [(ref, pieces.at[k]) for k, ref in enumerate(pieces_hbm)]
    first_pieces = started(piece_pairs[:4], semaphores, 0)
    slab_copies = started([(ref, slabs.at[k]) for k, ref in enumerate(slabs_hbm)], semaphores, 4)
    field_pairs = [(ref.at[:, SLAB : 2 * SLAB], fields.at[k]) for k, ref in enumerate(other_hbm)]
    field_copies = started(field_pairs, semaphores, 6)
    second_pieces = started(piece_pairs[4:], semaphores, 8)
    wait_for(first_pieces)
    unpack_sources(place_ref, [pieces.at[k] for k in range(4)], planes, source)
    wait_for(slab_copies)

    def keep_total(chip, near, base, terms):
        for p in range(planes):
            total[base + p] = terms[p]

    def finish(chip, near, base, terms):
        store_scaled(chip, near, [total[base + p] + terms[p] for p in range(planes)], keep_ref, send_ref)

    given = [slabs.at[k] for k in range(2)], source, [fields.at[k] for k in range(2)]
    given += (table_ref, double_ref), (first, second)
    solve_pair(place_ref[0], planes, *given, lambda: wait_for(field_copies), keep_total, nothing)
    wait_for(second_pieces)
    unpack_sources(place_ref, [pieces.at[k] for k in range(4, 8)], planes, source)
    solve_pair(place_ref[0], planes, *given, nothing, finish, nothing)


def solve_call(kernel, place, in_hbm, table, outs, out_spec, slabs, pairs):
    length = table.shape[0]
    whole = (length, length, LANES)
    hbm, vmem = pl.BlockSpec(memory_space=pl.ANY), pl.BlockSpec(memory_space=pltpu.VMEM)
    before, after = in_hbm
    section = pltpu.VMEM((2, (length + 1) * PITCH, LANES), F32)
    piece = (pairs * 4, length // 3, PIECE, ROWS, LANES)
    scratch = [pltpu.VMEM(shape, BF16) for shape in (*slabs, piece, (2,) + whole)]
    scratch += [section, section, pltpu.VMEM(whole, F32), pltpu.SemaphoreType.DMA((12,))]
    return pl.pallas_call(
        kernel,
        in_specs=[pl.BlockSpec(memory_space=pltpu.SMEM)] + [hbm] * len(before) + [vmem] * 2 + [hbm] * len(after),
        out_specs=[out_spec] * len(outs),
        out_shape=outs,
        scratch_shapes=scratch,
        compiler_params=pltpu.CompilerParams(vmem_limit_bytes=VMEM_LIMIT),
        cost_estimate=pl.CostEstimate(
            flops=144 * length**4 * pairs, bytes_accessed=8 * length**3, transcendentals=0
        ),
        name="solve",
    )(place, *before, table, double_table(table), *after)


def solve_first(place, orbital, pieces, table, before, planes):
    chips = orbital[0].shape[0]
    length = table.shape[0]
    last = before is not None
    out_spec = pl.BlockSpec(memory_space=pltpu.VMEM if last else pl.ANY)
    if last:
        outs = [jax.ShapeDtypeStruct((chips, SLAB, ROWS, LANES), kind) for kind in (F32, BF16)]
    else:
        outs = [jax.ShapeDtypeStruct((length, length, LANES), F32)]
    kernel = functools.partial(first_kernel, last, planes)
    in_hbm = ([*orbital, *pieces], [before] if last else [])
    return solve_call(kernel, place, in_hbm, table, outs, out_spec, [(2,) + orbital[0].shape], 1)


def solve_second(place, orbital, other, pieces, table, planes):
    shape = orbital[0].shape
    outs = [jax.ShapeDtypeStruct(shape, kind) for kind in (F32, BF16)]
    out_spec = pl.BlockSpec(memory_space=pltpu.VMEM)
    in_hbm = ([*orbital, *other, *pieces], [])
    kernel = functools.partial(second_kernel, planes)
    return solve_call(kernel, place, in_hbm, table, outs, out_spec, [(2,) + shape] * 2, 2)


def unpack_kernel(slab_ref, *refs):
    out_ref = refs[-1]
    planes, length = out_ref.shape[2:4]
    for chip in range(slab_ref.shape[0]):
        for p, plane in enumerate(slab_planes(slab_ref, chip, planes, length)):
            out_ref[chip, 0, p] = plane


def unpack_slabs(slabs, which, before, planes, length):
    chips = slabs.shape[0]
    steps = 2
    block = pl.BlockSpec((chips // steps,) + slabs.shape[1:], lambda i: (i, 0, 0, 0))
    given = [] if before is None else [before]
    return pl.pallas_call(
        unpack_kernel,
        grid=(steps,),
        in_specs=[block] + [pl.BlockSpec(memory_space=pl.ANY)] * len(given),
        out_specs=pl.BlockSpec((chips // steps, 1, planes, length, length), lambda i: (i, which, 0, 0, 0)),
        out_shape=jax.ShapeDtypeStruct((chips, 2, planes, length, length), BF16),
        input_output_aliases={1: 0} if given else {},
        compiler_params=pltpu.CompilerParams(vmem_limit_bytes=VMEM_LIMIT),
        name="unpack",
    )(slabs, *given)


def device(y, x, z, core):
    return ((y * 2 + x // 2) * 2 + x % 2) * 16 + z * 2 + core


def moved(value, dy=0, mirror=False, core=0):
    places = itertools.product(range(4), range(4), range(8), range(2))
    pairs = [(device(y, x, z, c), device((y + dy) % 4, 3 - x if mirror else x, z, c ^ core)) for y, x, z, c in places]
    return lax.ppermute(value, BOTH, pairs)


def between_chips(value):
    bands, parts = lax.axis_size("band"), lax.axis_size("pw")
    groups = [[b * parts + 2 * p + c for p in range(parts // 2)] for b in range(bands) for c in range(2)]
    return lax.all_to_all(value, BOTH, 0, 0, axis_index_groups=groups, tiled=True)


def own_kernel(me_ref, owners_ref, chosen_ref, orbitals_hbm, out_ref, slabs, semaphores):
    planes, length, width = slabs.shape[1:]
    copies = []
    for s in range(2):
        row = jnp.int32(0)
        for r in range(owners_ref.shape[0]):
            row = jnp.where(owners_ref[r] == me_ref[0], chosen_ref[r, s], row)
        copies.append(pltpu.make_async_copy(orbitals_hbm.at[row], slabs.at[s], semaphores.at[s]))
        copies[s].start()
    half = length // 2
    for s in range(2):
        copies[s].wait()
        for h in range(2):
            rows = slab_tiles([slabs[s, p, h * half : (h + 1) * half] for p in range(planes)])
            for t, tile in enumerate(packed_rows(rows, PIECE)):
                for band in range(h, out_ref.shape[0], 2):
                    out_ref[band, s, t] = tile


def own_pieces(orbitals, owners, chosen):
    me = lax.axis_index("band")
    bands = lax.axis_size("band")
    smem = pl.BlockSpec(memory_space=pltpu.SMEM)
    packed = pl.pallas_call(
        own_kernel,
        in_specs=[smem, smem, smem, pl.BlockSpec(memory_space=pl.ANY)],
        out_specs=pl.BlockSpec(memory_space=pltpu.VMEM),
        out_shape=jax.ShapeDtypeStruct((bands, 2, PIECE, ROWS, LANES), BF16),
        scratch_shapes=[pltpu.VMEM((2,) + orbitals.shape[1:], BF16), pltpu.SemaphoreType.DMA((2,))],
        name="own_pieces",
    )(me.reshape(1), owners, chosen, orbitals)
    received = lax.all_to_all(packed, "band", 0, 0, tiled=True)
    return lax.dynamic_index_in_dim(received, owners[me // 2], 0, keepdims=False)


def on_device(orbitals, owners, chosen, shell_index, shell_kernel):
    band, part = lax.axis_index("band"), lax.axis_index("pw")
    count, planes, length, width = orbitals.shape
    table = cas_table(length)
    place = jnp.stack([part % 2, band % 2])

    pieces = own_pieces(orbitals, owners, chosen)
    copies = jnp.broadcast_to(pieces[None], (count // 2,) + pieces.shape).reshape((count,) + pieces.shape[1:])
    own = lax.all_to_all(copies, "pw", 0, 0, tiled=True)
    across = moved(own, mirror=True)
    opposite = moved(own, dy=2)
    opposite_across = moved(opposite, mirror=True)
    later_own, _ = lax.optimization_barrier((own, opposite))
    beside = [moved(later_own, dy=dy) for dy in (1, 3)]

    slabs = list(pack_slabs(orbitals, jnp.swapaxes(shell_index, 0, 1), shell_kernel))
    even = between_chips(slabs[0])
    even, across, opposite_across, *beside = lax.optimization_barrier((even, across, opposite_across, *beside))
    beside_across = [moved(across, dy=dy) for dy in (1, 3)]
    even = (even, moved(even, core=1))
    slabs[1], _ = lax.optimization_barrier((slabs[1], across))
    odd = between_chips(slabs[1])
    odd = (odd, moved(odd, core=1))

    def finished(keep, send):
        return between_chips((keep + moved(send, core=1).astype(F32)).astype(BF16))

    pairs = [[own, across, opposite, opposite_across]]
    pairs.append([beside[0], beside_across[0], beside[1], beside_across[1]])
    (total,) = solve_first(place, even, pairs[0], table, None, planes)
    keep, send = solve_first(place, even, pairs[1], table, total, planes)
    result = unpack_slabs(finished(keep, send), 0, None, planes, length)
    later, _ = lax.optimization_barrier((pairs[0] + pairs[1], send))
    keep, send = solve_second(place, odd, even, later, table, planes)
    result = unpack_slabs(finished(keep, send), 1, result, planes, length)
    return result.reshape(orbitals.shape)


def solution(mesh):
    return jax.shard_map(
        on_device,
        mesh=mesh,
        in_specs=(P("band", "pw", None, None), P(), P(), P(None, "pw", None), P()),
        out_specs=P("band", "pw", None, None),
        check_vma=False,
    )
```

```python
import functools
import itertools
import math

import jax
import jax.numpy as jnp
import ml_dtypes
import numpy as np
from jax import lax
from jax.experimental import pallas as pl
from jax.experimental.pallas import tpu as pltpu
from jax.sharding import PartitionSpec as P

F32 = jnp.float32
BF16 = jnp.bfloat16
EXCHANGE_FRACTION = 0.25
LANES = 128
ROWS = 16
SLAB = 14
PIECE = 7
VMEM_LIMIT = 49 * 2**20
SMALL_LIMIT = 16 * 2**20
PITCH = 104
CHIP_GROUP = 8
BOTH = ("band", "pw")
HALVES = (slice(0, LANES), slice(LANES, 2 * LANES))


def cas_table(length):
    counter = np.arange(length)
    angles = counter[:, None] * counter[None, :] % length * (2.0 * math.pi / length)
    return ((np.cos(angles) + np.sin(angles)) / math.sqrt(length)).astype(ml_dtypes.bfloat16)


def double_table(table):
    length = table.shape[0]
    wide = np.zeros((2 * LANES, 2 * LANES), table.dtype)
    for low in (0, LANES):
        wide[low : low + length, low : low + length] = table
    return wide


def dot(a, b):
    return jnp.dot(a, b, preferred_element_type=F32)


def packed_rows(rows, kept):
    width = rows[0].shape[1]
    free = LANES - width
    thirds = [rows[kept + k // 3][:, (k % 3) * free : (k % 3 + 1) * free] for k in range(3 * (len(rows) - kept))]
    thirds += [jnp.zeros_like(thirds[0])] * (kept - len(thirds))
    return [jnp.concatenate([rows[t], thirds[t]], axis=1) for t in range(kept)]


def unpacked_rows(tiles, count, width):
    extra = count - len(tiles)
    spare = [jnp.concatenate([tiles[3 * j + k][:, width:] for k in range(3)], axis=1) for j in range(extra)]
    return [t[:, :width] for t in tiles] + spare


def slab_planes(ref, chip, planes, length):
    per_plane = length // ROWS
    rows = unpacked_rows([ref[chip, t] for t in range(SLAB)], planes * per_plane, length)
    return [jnp.concatenate(rows[p * per_plane : (p + 1) * per_plane], axis=0) for p in range(planes)]


def slab_tiles(planes):
    return [plane[t * ROWS : (t + 1) * ROWS] for plane in planes for t in range(plane.shape[0] // ROWS)]


def pack_kernel(orbital_ref, index_ref, values_ref, even_ref, odd_ref):
    planes, length, width = index_ref.shape
    values = jnp.broadcast_to(values_ref[...], (length, LANES))
    blank = jnp.zeros((length, LANES - width), jnp.int32)
    field = []
    for plane in range(planes):
        levels = jnp.concatenate([index_ref[plane], blank], axis=1)
        here = jnp.take_along_axis(values, levels, axis=1, mode="promise_in_bounds")
        field.append(here[:, :width].astype(BF16))
    field = packed_rows(slab_tiles(field), SLAB)
    chips = even_ref.shape[0]
    unroll = 4

    @pl.loop(0, chips // unroll)
    def _(step):
        for k in range(unroll):
            chip = step * unroll + k
            for which, ref in enumerate((even_ref, odd_ref)):
                slab = [orbital_ref[2 * chip + which, p] for p in range(planes)]
                for t, tile in enumerate(packed_rows(slab_tiles(slab), SLAB)):
                    ref[chip, t] = tile
            for t in range(SLAB):
                even_ref[chip, SLAB + t] = field[t]


def pack_slabs(orbitals, shell_index, shell_kernel):
    chips = orbitals.shape[0] // 2
    vmem = pl.BlockSpec(memory_space=pltpu.VMEM)
    return pl.pallas_call(
        pack_kernel,
        in_specs=[vmem] * 3,
        out_specs=[vmem] * 2,
        out_shape=[jax.ShapeDtypeStruct((chips, n * SLAB, ROWS, LANES), BF16) for n in (2, 1)],
        compiler_params=pltpu.CompilerParams(vmem_limit_bytes=SMALL_LIMIT),
        name="pack",
    )(orbitals, shell_index, shell_kernel.reshape(1, LANES))


def unpack_sources(place_ref, pieces, planes, source):
    length = source.shape[1]
    per_plane = length // 2 // ROWS
    blank = jnp.zeros((length // 2, LANES - length), BF16)
    lows = [pl.multiple_of(h * (length // 2), ROWS) for h in (place_ref[1], 1 - place_ref[1])]
    unroll = 8

    @pl.loop(0, length // planes // unroll)
    def _(step):
        for k in range(unroll):
            part = step * unroll + k
            for number, ref in enumerate(pieces):
                rows = unpacked_rows([ref[part, t] for t in range(PIECE)], planes * per_plane, length)
                for plane in range(planes):
                    here = jnp.concatenate(rows[per_plane * plane : per_plane * (plane + 1)], axis=0)
                    here = jnp.concatenate([here, blank], axis=1)
                    source[number // 2, part * planes + plane, pl.ds(lows[number % 2], length // 2), :] = here


def solve_pair(core, planes, orbital, source, fields, tables, scratch, wait_fields, finish, step_done):
    near_ref, far_ref = orbital
    table_ref, double_ref = tables
    first, second = scratch
    chips = near_ref.shape[0]
    length = table_ref.shape[0]
    table = table_ref[...]
    blank = jnp.zeros((length, LANES - length), BF16)

    def slabs_of(step):
        for k in range(CHIP_GROUP):
            for near in (True, False):
                chip = step * CHIP_GROUP + k
                yield chip, near, (2 * chip + (core if near else 1 - core)) * planes

    @pl.loop(0, chips // CHIP_GROUP)
    def _(step):
        rows = []
        for chip, near, base in slabs_of(step):
            for p, plane in enumerate(slab_planes(near_ref if near else far_ref, chip, planes, length)):
                plane = jnp.concatenate([plane, blank], axis=1).astype(F32)
                pair = [(source[s, base + p].astype(F32) * plane).astype(BF16) for s in range(2)]
                rows.append(jnp.concatenate(pair, axis=1))
        along_z = dot(jnp.concatenate(rows, axis=0), double_ref[...]).astype(BF16)
        for k, (chip, near, base) in enumerate(slabs_of(step)):
            for p in range(planes):
                low = (k * planes + p) * length
                section = dot(table, along_z[low : low + length])
                at = pl.multiple_of((base + p) * PITCH, 8)
                for s in range(2):
                    first[s, pl.ds(at, length), :] = section[:, HALVES[s]]

    wait_fields()

    @pl.loop(0, chips // CHIP_GROUP)
    def _(step):
        for chip, near, base in slabs_of(step):
            for p, field in enumerate(slab_planes(fields[0] if near else fields[1], chip, planes, length)):
                field = jnp.concatenate([field, blank], axis=1).astype(F32)
                row = base + p
                values = [first[s, pl.ds(row, length, stride=PITCH), :].astype(BF16) for s in range(2)]
                section = dot(table, jnp.concatenate(values, axis=1))
                values = [(section[:, HALVES[s]] * field).astype(BF16) for s in range(2)]
                section = dot(table, jnp.concatenate(values, axis=1))
                at = pl.multiple_of(row * PITCH, 8)
                for s in range(2):
                    second[s, pl.ds(at, length), :] = section[:, HALVES[s]]

    @pl.loop(0, chips // CHIP_GROUP)
    def _(step):
        sections = []
        for chip, near, base in slabs_of(step):
            for p in range(planes):
                values = [second[s, pl.ds(base + p, length, stride=PITCH), :].astype(BF16) for s in range(2)]
                sections.append(dot(table, jnp.concatenate(values, axis=1)).astype(BF16))
        potential = dot(jnp.concatenate(sections, axis=0), double_ref[...])
        for k, (chip, near, base) in enumerate(slabs_of(step)):
            terms = []
            for p in range(planes):
                low = (k * planes + p) * length
                here = potential[low : low + length]
                both = [source[s, base + p].astype(F32) * here[:, HALVES[s]] for s in range(2)]
                terms.append(both[0] + both[1])
            finish(chip, near, base, terms)
        step_done(step)


def store_scaled(chip, near, sums, keep_ref, send_ref):
    length = sums[0].shape[0]
    rows = slab_tiles([(-EXCHANGE_FRACTION * value)[:, :length] for value in sums])
    for t, tile in enumerate(packed_rows(rows, SLAB)):
        if near:
            keep_ref[chip, t] = tile
        else:
            send_ref[chip, t] = tile.astype(BF16)


def started(pairs, semaphores, low):
    copies = [pltpu.make_async_copy(*pair, semaphores.at[low + k]) for k, pair in enumerate(pairs)]
    for copy in copies:
        copy.start()
    return copies


def wait_for(copies):
    for copy in copies:
        copy.wait()


def nothing(*_):
    pass


def first_kernel(last, planes, place_ref, *refs):
    slabs_hbm, pieces_hbm, (table_ref, double_ref), refs = refs[:2], refs[2:6], refs[6:8], refs[8:]
    if last:
        before_hbm, keep_ref, send_ref, *refs = refs
    else:
        total_hbm, *refs = refs
    slabs, pieces, source, first, second, total, semaphores = refs
    piece_copies = started([(ref, pieces.at[k]) for k, ref in enumerate(pieces_hbm)], semaphores, 0)
    slab_copies = started([(ref, slabs.at[k]) for k, ref in enumerate(slabs_hbm)], semaphores, 4)
    if last:
        total_copies = started([(before_hbm, total)], semaphores, 6)
    wait_for(piece_copies)
    unpack_sources(place_ref, [pieces.at[k] for k in range(4)], planes, source)
    wait_for(slab_copies)
    chunk = CHIP_GROUP * 2 * planes

    def rows_out(step):
        rows = pl.ds(pl.multiple_of(step * chunk, chunk), chunk)
        return pltpu.make_async_copy(total.at[rows], total_hbm.at[rows], semaphores.at[6 + step])

    def wait_fields():
        if last:
            wait_for(total_copies)

    def finish(chip, near, base, terms):
        if last:
            sums = [total[base + p] + terms[p] for p in range(planes)]
            store_scaled(chip, near, sums, keep_ref, send_ref)
        else:
            for p in range(planes):
                total[base + p] = terms[p]

    def step_done(step):
        if not last:
            rows_out(step).start()

    orbital = [slabs.at[k, :, 0:SLAB] for k in range(2)]
    fields = [slabs.at[k, :, SLAB : 2 * SLAB] for k in range(2)]
    tables, scratch = (table_ref, double_ref), (first, second)
    solve_pair(place_ref[0], planes, orbital, source, fields, tables, scratch, wait_fields, finish, step_done)
    if not last:
        for step in range(total.shape[0] // chunk):
            rows_out(step).wait()


def second_kernel(planes, place_ref, *refs):
    slabs_hbm, other_hbm, pieces_hbm, (table_ref, double_ref), refs = refs[:2], refs[2:4], refs[4:12], refs[12:14], refs[14:]
    keep_ref, send_ref, slabs, fields, pieces, source, first, second, total, semaphores = refs
    piece_pairs = [(ref, pieces.at[k]) for k, ref in enumerate(pieces_hbm)]
    first_pieces = started(piece_pairs[:4], semaphores, 0)
    slab_copies = started([(ref, slabs.at[k]) for k, ref in enumerate(slabs_hbm)], semaphores, 4)
    field_pairs = [(ref.at[:, SLAB : 2 * SLAB], fields.at[k]) for k, ref in enumerate(other_hbm)]
    field_copies = started(field_pairs, semaphores, 6)
    second_pieces = started(piece_pairs[4:], semaphores, 8)
    wait_for(first_pieces)
    unpack_sources(place_ref, [pieces.at[k] for k in range(4)], planes, source)
    wait_for(slab_copies)

    def keep_total(chip, near, base, terms):
        for p in range(planes):
            total[base + p] = terms[p]

    def finish(chip, near, base, terms):
        store_scaled(chip, near, [total[base + p] + terms[p] for p in range(planes)], keep_ref, send_ref)

    given = [slabs.at[k] for k in range(2)], source, [fields.at[k] for k in range(2)]
    given += (table_ref, double_ref), (first, second)
    solve_pair(place_ref[0], planes, *given, lambda: wait_for(field_copies), keep_total, nothing)
    wait_for(second_pieces)
    unpack_sources(place_ref, [pieces.at[k] for k in range(4, 8)], planes, source)
    solve_pair(place_ref[0], planes, *given, nothing, finish, nothing)


def solve_call(kernel, place, in_hbm, table, outs, out_spec, slabs, pairs):
    length = table.shape[0]
    whole = (length, length, LANES)
    hbm, vmem = pl.BlockSpec(memory_space=pl.ANY), pl.BlockSpec(memory_space=pltpu.VMEM)
    before, after = in_hbm
    section = pltpu.VMEM((2, (length + 1) * PITCH, LANES), F32)
    piece = (pairs * 4, length // 3, PIECE, ROWS, LANES)
    scratch = [pltpu.VMEM(shape, BF16) for shape in (*slabs, piece, (2,) + whole)]
    scratch += [section, section, pltpu.VMEM(whole, F32), pltpu.SemaphoreType.DMA((12,))]
    return pl.pallas_call(
        kernel,
        in_specs=[pl.BlockSpec(memory_space=pltpu.SMEM), *[hbm] * len(before), vmem, vmem] + [hbm] * len(after),
        out_specs=[out_spec] * len(outs),
        out_shape=outs,
        scratch_shapes=scratch,
        compiler_params=pltpu.CompilerParams(vmem_limit_bytes=VMEM_LIMIT),
        cost_estimate=pl.CostEstimate(
            flops=144 * length**4 * pairs, bytes_accessed=8 * length**3, transcendentals=0
        ),
        name="solve",
    )(place, *before, table, double_table(table), *after)


def solve_first(place, orbital, pieces, table, before, planes):
    chips = orbital[0].shape[0]
    length = table.shape[0]
    last = before is not None
    out_spec = pl.BlockSpec(memory_space=pltpu.VMEM if last else pl.ANY)
    if last:
        outs = [jax.ShapeDtypeStruct((chips, SLAB, ROWS, LANES), kind) for kind in (F32, BF16)]
    else:
        outs = [jax.ShapeDtypeStruct((length, length, LANES), F32)]
    kernel = functools.partial(first_kernel, last, planes)
    in_hbm = ([*orbital, *pieces], [before] if last else [])
    return solve_call(kernel, place, in_hbm, table, outs, out_spec, [(2,) + orbital[0].shape], 1)


def solve_second(place, orbital, other, pieces, table, planes):
    shape = orbital[0].shape
    outs = [jax.ShapeDtypeStruct(shape, kind) for kind in (F32, BF16)]
    out_spec = pl.BlockSpec(memory_space=pltpu.VMEM)
    in_hbm = ([*orbital, *other, *pieces], [])
    kernel = functools.partial(second_kernel, planes)
    return solve_call(kernel, place, in_hbm, table, outs, out_spec, [(2,) + shape] * 2, 2)


def unpack_kernel(steps, slabs_ref, *refs):
    out_ref = refs[-1]
    planes, length = out_ref.shape[2:4]
    chips = slabs_ref.shape[0] // steps
    step = pl.program_id(0)
    for k in range(steps):

        @pl.when(step == k)
        def _():
            for chip in range(chips):
                for p, plane in enumerate(slab_planes(slabs_ref, k * chips + chip, planes, length)):
                    out_ref[chip, 0, p] = plane


def unpack_slabs(slabs, which, before, planes, length):
    chips = slabs.shape[0]
    steps = 2
    given = [] if before is None else [before]
    return pl.pallas_call(
        functools.partial(unpack_kernel, steps),
        grid=(steps,),
        in_specs=[pl.BlockSpec(memory_space=pltpu.VMEM)] + [pl.BlockSpec(memory_space=pl.ANY)] * len(given),
        out_specs=pl.BlockSpec((chips // steps, 1, planes, length, length), lambda i: (i, which, 0, 0, 0)),
        out_shape=jax.ShapeDtypeStruct((chips, 2, planes, length, length), BF16),
        input_output_aliases={1: 0} if given else {},
        compiler_params=pltpu.CompilerParams(vmem_limit_bytes=SMALL_LIMIT),
        name="unpack",
    )(slabs, *given)


def device(y, x, z, core):
    return ((y * 2 + x // 2) * 2 + x % 2) * 16 + z * 2 + core


def moved(value, dy=0, mirror=False, core=0):
    places = itertools.product(range(4), range(4), range(8), range(2))
    pairs = [(device(y, x, z, c), device((y + dy) % 4, 3 - x if mirror else x, z, c ^ core)) for y, x, z, c in places]
    return lax.ppermute(value, BOTH, pairs)


def between_chips(value):
    bands, parts = lax.axis_size("band"), lax.axis_size("pw")
    groups = [[b * parts + 2 * p + c for p in range(parts // 2)] for b in range(bands) for c in range(2)]
    return lax.all_to_all(value, BOTH, 0, 0, axis_index_groups=groups, tiled=True)


def own_kernel(place_ref, owners_ref, chosen_ref, orbitals_hbm, out_ref, slabs, semaphores):
    planes, length, width = slabs.shape[1:]
    copies = []
    for s in range(2):
        row = jnp.int32(0)
        for r in range(owners_ref.shape[0]):
            row = jnp.where(owners_ref[r] == place_ref[2], chosen_ref[r, s], row)
        copies.append(pltpu.make_async_copy(orbitals_hbm.at[row], slabs.at[s], semaphores.at[s]))
        copies[s].start()
    half = length // 2
    for s in range(2):
        copies[s].wait()
        for h in range(2):
            rows = slab_tiles([slabs[s, p, h * half : (h + 1) * half] for p in range(planes)])
            for t, tile in enumerate(packed_rows(rows, PIECE)):
                for band in range(h, out_ref.shape[0], 2):
                    out_ref[band, s, t] = tile


def own_pieces(place, orbitals, owners, chosen):
    me = lax.axis_index("band")
    bands = lax.axis_size("band")
    smem = pl.BlockSpec(memory_space=pltpu.SMEM)
    packed = pl.pallas_call(
        own_kernel,
        in_specs=[smem, smem, smem, pl.BlockSpec(memory_space=pl.ANY)],
        out_specs=pl.BlockSpec(memory_space=pltpu.VMEM),
        out_shape=jax.ShapeDtypeStruct((bands, 2, PIECE, ROWS, LANES), BF16),
        scratch_shapes=[pltpu.VMEM((2,) + orbitals.shape[1:], BF16), pltpu.SemaphoreType.DMA((2,))],
        name="own_pieces",
    )(place, owners, chosen, orbitals)
    received = lax.all_to_all(packed, "band", 0, 0, tiled=True)
    return lax.dynamic_index_in_dim(received, owners[me // 2], 0, keepdims=False)


def on_device(orbitals, owners, chosen, shell_index, shell_kernel):
    band, part = lax.axis_index("band"), lax.axis_index("pw")
    count, planes, length, width = orbitals.shape
    table = cas_table(length)
    place = jnp.stack([part % 2, band % 2, band])

    pieces = own_pieces(place, orbitals, owners, chosen)
    copies = jnp.broadcast_to(pieces[None], (count // 2,) + pieces.shape).reshape((count,) + pieces.shape[1:])
    own = lax.all_to_all(copies, "pw", 0, 0, tiled=True)
    across = moved(own, mirror=True)
    opposite = moved(own, dy=2)
    opposite_across = moved(opposite, mirror=True)
    later_own, _ = lax.optimization_barrier((own, opposite))
    beside = [moved(later_own, dy=dy) for dy in (1, 3)]

    slabs = list(pack_slabs(orbitals, jnp.swapaxes(shell_index, 0, 1), shell_kernel))
    even = between_chips(slabs[0])
    even, across, opposite_across, *beside = lax.optimization_barrier((even, across, opposite_across, *beside))
    beside_across = [moved(across, dy=dy) for dy in (1, 3)]
    even = (even, moved(even, core=1))
    slabs[1], _ = lax.optimization_barrier((slabs[1], across))
    odd = between_chips(slabs[1])
    odd = (odd, moved(odd, core=1))

    def finished(keep, send):
        return between_chips((keep + moved(send, core=1).astype(F32)).astype(BF16))

    pairs = [[own, across, opposite, opposite_across]]
    pairs.append([beside[0], beside_across[0], beside[1], beside_across[1]])
    (total,) = solve_first(place, even, pairs[0], table, None, planes)
    keep, send = solve_first(place, even, pairs[1], table, total, planes)
    result = unpack_slabs(finished(keep, send), 0, None, planes, length)
    later, _ = lax.optimization_barrier((pairs[0] + pairs[1], send))
    keep, send = solve_second(place, odd, even, later, table, planes)
    result = unpack_slabs(finished(keep, send), 1, result, planes, length)
    return result.reshape(orbitals.shape)


def solution(mesh):
    return jax.shard_map(
        on_device,
        mesh=mesh,
        in_specs=(P("band", "pw", None, None), P(), P(), P(None, "pw", None), P()),
        out_specs=P("band", "pw", None, None),
        check_vma=False,
    )
```
